256 devices in a mesh: blk: 16 (over y_hi, x, core), head: 16 (over z, y_lo).
Axes of the slice: x: 4, y: 4 (y_hi: 2, y_lo: 2; y = y_hi * 2 + y_lo), z: 8, core: 2. Of those that a mesh axis runs over, the one named last changes fastest.
Arguments:
- queries: bfloat16 [32768, 4096], P(('blk', 'head')), may hold values from -6 to 6
- key_matrix: bfloat16 [32768, 512], P(('blk', 'head')), may hold values from -6 to 6
- value_matrix: bfloat16 [32768, 512], P(('blk', 'head')), may hold values from -6 to 6
- saved_output: bfloat16 [32768, 4096], P(('blk', 'head')), may hold values from -4 to 4
- output_gradient: bfloat16 [32768, 4096], P(('blk', 'head')), may hold values from -96 to 96
- saved_logsumexp: float32 [32768, 32], P(('blk', 'head')), may hold values from -1 to 16
- block_order: int32 [32], replicated, may hold values from 0 to 31, as said below
Outputs:
- query_grad: float32 [32768, 4096], P(('blk', 'head'))
- key_gradient: float32 [32768, 512], P(('blk', 'head'))
- value_gradient: float32 [32768, 512], P(('blk', 'head'))
The draws below stay inside these ranges and needn't reach their ends.
Inputs may be any that keep to these rules, and one draw needn't show every extreme that they name: `block_order`: a permutation of 0 to 31.
All inputs are finite; a program needn't handle non-finite values.
Results may differ from the reference program's by a relative error of at most 0.0028.
Values may be sent and summed in bfloat16 or wider, within the bound.
A program may use at most 192 MiB of HBM per device.

```python
import jax
import jax.numpy as jnp
from jax import lax

QUERY_HEADS = 32
KEY_VALUE_HEADS = 4
HEAD_FEATURES = 128
WINDOW_ROUNDS = 2
BLOCK_ROWS = 2048
SEGMENT_TOKENS = 1024
SEGMENT_COUNT = 32
TOKEN_COUNT = 32768


def shared_order(key):
    return jax.random.permutation(key, SEGMENT_COUNT).astype(jnp.int32)


def draw_block_order(key, part):
    return shared_order(key)


def draw_saved_logsumexp(key, part):
    block_order = shared_order(key)
    key = jax.random.fold_in(key, 11)
    token = jnp.arange(TOKEN_COUNT, dtype=jnp.int32)
    segment = token // SEGMENT_TOKENS
    position = block_order[segment] * SEGMENT_TOKENS + token % SEGMENT_TOKENS
    home_block = segment // 2
    visible = jnp.zeros((TOKEN_COUNT,), jnp.int32)
    for round_index in range(WINDOW_ROUNDS):
        source = (2 * home_block - round_index) % SEGMENT_COUNT
        start = block_order[source] * SEGMENT_TOKENS
        visible = visible + jnp.clip(position - start + 1, 0, SEGMENT_TOKENS)
    visible = jnp.maximum(visible, 1)
    offset = jax.random.uniform(key, (TOKEN_COUNT, QUERY_HEADS), jnp.float32, -0.5, 1.0)
    return (jnp.log(visible.astype(jnp.float32))[:, None] + offset).astype(jnp.float32)


def block_scale(rng, shape, cuts, smallest, high):
    def one(dim, parts):
        steps = jax.random.uniform(jax.random.fold_in(jax.random.fold_in(rng, 6), dim), (parts,), jnp.float32, smallest / len(cuts), high / len(cuts))
        return jnp.repeat(jnp.exp(steps), shape[dim] // parts).reshape((-1,) + (1,) * (len(shape) - dim - 1))

    factor_of = one(*cuts[0])
    for cut in cuts[1:]:
        factor_of = factor_of * one(*cut)
    return factor_of


def noise(rng, dims, scale, bound, split=(), held_as=jnp.bfloat16):
    array = scale * jax.random.normal(rng, dims, jnp.float32)
    if split:
        array = array * block_scale(rng, dims, split, -0.22, 0.18)
    return jnp.clip(array, -bound, bound).astype(held_as)


def setup_inputs(seed: int = 0) -> dict:
    streams_of = jax.random.split(jax.random.key(seed), 8)
    return {
        "queries": noise(streams_of[0], (TOKEN_COUNT, QUERY_HEADS * HEAD_FEATURES), 1.0, 6.0, ((0, 256),)),
        "key_matrix": noise(streams_of[1], (TOKEN_COUNT, KEY_VALUE_HEADS * HEAD_FEATURES), 1.0, 6.0, ((0, 256),)),
        "value_matrix": noise(streams_of[2], (TOKEN_COUNT, KEY_VALUE_HEADS * HEAD_FEATURES), 1.0, 6.0, ((0, 256),)),
        "saved_output": noise(streams_of[3], (TOKEN_COUNT, QUERY_HEADS * HEAD_FEATURES), 0.3, 4.0, ((0, 256),)),
        "output_gradient": noise(streams_of[4], (TOKEN_COUNT, QUERY_HEADS * HEAD_FEATURES), 16.0, 96.0, ((0, 256),)),
        "saved_logsumexp": draw_saved_logsumexp(jax.random.fold_in(streams_of[7], 71), 0),
        "block_order": draw_block_order(jax.random.fold_in(streams_of[7], 71), 0),
    }


def reference(queries, key_matrix, value_matrix, saved_output, output_gradient, saved_logsumexp, block_order):
    block_grand_sum = SEGMENT_COUNT // 2
    query_group = QUERY_HEADS // KEY_VALUE_HEADS
    scaling = HEAD_FEATURES ** -0.5
    highest = lax.Precision.HIGHEST
    token = jnp.arange(TOKEN_COUNT, dtype=jnp.int32)
    position = (block_order[token // SEGMENT_TOKENS] * SEGMENT_TOKENS + token % SEGMENT_TOKENS).astype(jnp.int32)
    block_pos = position.reshape(block_grand_sum, BLOCK_ROWS)
    seg_pos = position.reshape(SEGMENT_COUNT, SEGMENT_TOKENS)
    row_correction = jnp.sum((output_gradient.astype(jnp.float32) * saved_output.astype(jnp.float32)).reshape(TOKEN_COUNT, QUERY_HEADS, HEAD_FEATURES), axis=2)
    query_grid5 = queries.reshape(block_grand_sum, BLOCK_ROWS, KEY_VALUE_HEADS, query_group, HEAD_FEATURES)
    output_grad5 = output_gradient.reshape(block_grand_sum, BLOCK_ROWS, KEY_VALUE_HEADS, query_group, HEAD_FEATURES)
    key_grid4 = key_matrix.reshape(SEGMENT_COUNT, SEGMENT_TOKENS, KEY_VALUE_HEADS, HEAD_FEATURES)
    value_grid4 = value_matrix.reshape(SEGMENT_COUNT, SEGMENT_TOKENS, KEY_VALUE_HEADS, HEAD_FEATURES)
    logsumexp_grid4 = saved_logsumexp.reshape(block_grand_sum, BLOCK_ROWS, KEY_VALUE_HEADS, query_group)
    delta_grid4 = row_correction.reshape(block_grand_sum, BLOCK_ROWS, KEY_VALUE_HEADS, query_group)

    def per_block(block_id):
        sources = [((2 * block_id - round_index) % SEGMENT_COUNT).astype(jnp.int32) for round_index in range(WINDOW_ROUNDS)]
        key_window = jnp.concatenate([key_grid4[source] for source in sources], axis=0)
        value_window = jnp.concatenate([value_grid4[source] for source in sources], axis=0)
        key_pos = jnp.concatenate([seg_pos[source] for source in sources], axis=0)
        causal = block_pos[block_id][:, None] >= key_pos[None, :]

        def per_head(pieces):
            head_query, head_dout, head_key, head_value, head_lse, head_delta = pieces
            query_wide = head_query.astype(jnp.float32)
            dout_wide = head_dout.astype(jnp.float32)
            key_wide = head_key.astype(jnp.float32)
            value_wide = head_value.astype(jnp.float32)
            scores = jnp.einsum("qhd,kd->hqk", query_wide, key_wide, precision=highest) * scaling
            weights = jnp.where(causal[None], jnp.exp(scores - head_lse.T[:, :, None]), 0.0)
            prob_grad = jnp.einsum("qhd,kd->hqk", dout_wide, value_wide, precision=highest)
            score_grad = weights * (prob_grad - head_delta.T[:, :, None])
            weights_low = lax.optimization_barrier(weights.astype(jnp.bfloat16)).astype(jnp.float32)
            grad_low = lax.optimization_barrier(score_grad.astype(jnp.bfloat16)).astype(jnp.float32)
            value_partial = jnp.einsum("hqk,qhd->kd", weights_low, dout_wide, precision=highest)
            key_partial = jnp.einsum("hqk,qhd->kd", grad_low, query_wide, precision=highest) * scaling
            query_part = jnp.einsum("hqk,kd->qhd", grad_low, key_wide, precision=highest) * scaling
            return query_part, key_partial, value_partial

        query_part, key_partial, value_partial = lax.map(per_head, (
            jnp.moveaxis(query_grid5[block_id], 1, 0),
            jnp.moveaxis(output_grad5[block_id], 1, 0),
            jnp.moveaxis(key_window, 1, 0),
            jnp.moveaxis(value_window, 1, 0),
            jnp.moveaxis(logsumexp_grid4[block_id], 1, 0),
            jnp.moveaxis(delta_grid4[block_id], 1, 0)))
        query_part = jnp.moveaxis(query_part, 0, 1).reshape(BLOCK_ROWS, QUERY_HEADS * HEAD_FEATURES)
        key_partial = jnp.moveaxis(key_partial, 0, 1).reshape(WINDOW_ROUNDS, SEGMENT_TOKENS, KEY_VALUE_HEADS * HEAD_FEATURES)
        value_partial = jnp.moveaxis(value_partial, 0, 1).reshape(WINDOW_ROUNDS, SEGMENT_TOKENS, KEY_VALUE_HEADS * HEAD_FEATURES)
        return query_part, key_partial, value_partial

    query_all, key_parts, value_parts = lax.map(per_block, jnp.arange(block_grand_sum, dtype=jnp.int32))
    query_grad = query_all.reshape(TOKEN_COUNT, QUERY_HEADS * HEAD_FEATURES)
    key_grand_sum = jnp.zeros((SEGMENT_COUNT, SEGMENT_TOKENS, KEY_VALUE_HEADS * HEAD_FEATURES), jnp.float32)
    value_grand_sum = jnp.zeros((SEGMENT_COUNT, SEGMENT_TOKENS, KEY_VALUE_HEADS * HEAD_FEATURES), jnp.float32)
    block_ids = jnp.arange(block_grand_sum, dtype=jnp.int32)
    for round_index in range(WINDOW_ROUNDS):
        targets = ((2 * block_ids - round_index) % SEGMENT_COUNT).astype(jnp.int32)
        key_grand_sum = key_grand_sum.at[targets].add(key_parts[:, round_index])
        value_grand_sum = value_grand_sum.at[targets].add(value_parts[:, round_index])
    key_gradient = key_grand_sum.reshape(TOKEN_COUNT, KEY_VALUE_HEADS * HEAD_FEATURES)
    value_gradient = value_grand_sum.reshape(TOKEN_COUNT, KEY_VALUE_HEADS * HEAD_FEATURES)
    return (query_grad, key_gradient, value_gradient)
```

```python
import functools

import jax
import jax.numpy as jnp
from jax import lax
from jax.experimental import pallas as pl
from jax.experimental.pallas import tpu as pltpu
from jax.sharding import PartitionSpec as P

F32 = jnp.float32
BF16 = jnp.bfloat16
FEAT = 128
SCALE = FEAT**-0.5
LOG2E = 1.4426950408889634
UNSEEN = 1e30
MESH = pl.DeviceIdType.MESH


def dot(a, b, ca, cb):
    return lax.dot_general(a, b, (((ca,), (cb,)), ((), ())), preferred_element_type=F32)


def span(start, size):
    return pl.ds(pl.multiple_of(start, size), size)


def kernel(
    order, q_hbm, k_hbm, v_hbm, o_hbm, do_hbm, lse_ref, dq_hbm, dk_hbm, dv_hbm,
    q_s, do_s, kv_s, o_full, do_full, st_own, st_s, aux, mask_s, ps, dss, dq_t, dkv,
    rs_in, rs_out, fin, dq_out, dq_in, dq_stage,
    sem_full, sem_ql, sem_qr, sem_qs, sem_st, sem_ar, sem_as, sem_gr, sem_gs, sem_rr, sem_rs,
    sem_fr, sem_fs, sem_dqr, sem_dqs, sem_out,
):
    b = lax.axis_index("blk")
    hd = lax.axis_index("head")
    z = hd // 2
    y = hd % 2
    yo = 1 - y
    partner = (b, 2 * z + yo)
    ring = ((b, (hd + 2) % 16), (b, (hd + 14) % 16))
    nxt = (b + 1) % 16
    prv = (b + 15) % 16
    first_half = z < 4

    barrier = pltpu.get_barrier_semaphore()
    peers = [partner, ring[0], ring[1], (nxt, hd), (prv, hd), (nxt, 2 * z + yo), (prv, 2 * z + yo)]
    for peer in peers:
        pl.semaphore_signal(barrier, inc=1, device_id=peer, device_id_type=MESH)

    def local_q(a, t):
        src, dst = ((q_hbm, q_s), (do_hbm, do_s))[t]

        def one(h, c):
            pltpu.make_async_copy(
                src.at[:, span((16 * y + 8 * a + h) * FEAT, FEAT)], dst.at[a, y, h], sem_ql.at[a, t]
            ).start()
            return c

        lax.fori_loop(0, 8, one, 0)

    full_o = pltpu.make_async_copy(o_hbm, o_full, sem_full.at[0])
    full_do = pltpu.make_async_copy(do_hbm, do_full, sem_full.at[1])
    full_o.start()
    full_do.start()
    for a in range(2):
        for t in range(2):
            local_q(a, t)
    pl.semaphore_wait(barrier, len(peers))

    def remote(src, dst, ss, rs, dev):
        return pltpu.make_async_remote_copy(
            src_ref=src, dst_ref=dst, send_sem=ss, recv_sem=rs, device_id=dev, device_id_type=MESH
        )

    bt = jnp.where(first_half, b, nxt)
    for a in range(2):
        for kv, ref in enumerate((k_hbm, v_hbm)):
            dst = kv_s.at[a, z, kv, span(y * FEAT, FEAT)]
            far = ref.at[:, span((2 * yo + a) * FEAT, FEAT)]
            near = ref.at[:, span((2 * y + a) * FEAT, FEAT)]
            remote(far, dst, sem_as.at[0, a, kv], sem_ar.at[a, kv, y], (bt, 2 * z + yo)).start()

            @pl.when(first_half)
            def _():
                pltpu.make_async_copy(near, dst, sem_ar.at[a, kv, y]).start()

            @pl.when(jnp.logical_not(first_half))
            def _():
                remote(near, dst, sem_as.at[1, a, kv], sem_ar.at[a, kv, y], (bt, hd)).start()

    for a in range(2):
        for t, (src, dst) in enumerate(((q_hbm, q_s), (do_hbm, do_s))):

            def one(h, c):
                remote(
                    src.at[:, span((16 * yo + 8 * a + h) * FEAT, FEAT)], dst.at[a, y, h],
                    sem_qs.at[a, t], sem_qr.at[a, t], partner,
                ).start()
                return c

            lax.fori_loop(0, 8, one, 0)

    def gather_copy(d, a, s):
        j = (z + 8 - s) % 8 if d == 0 else (z + s) % 8
        return remote(
            kv_s.at[a, j], kv_s.at[a, j], sem_gs.at[d, a, s], sem_gr.at[d, a, s], ring[d]
        )

    def gather_wait(d, a, s):
        gather_copy(d, a, s).wait_recv()

    for a in range(2):
        for kv in range(2):
            for half in range(2):
                place = kv_s.at[a, z, kv, pl.ds(half * FEAT, FEAT)]
                pltpu.make_async_copy(place, place, sem_ar.at[a, kv, half]).wait()
        for d in range(2):
            gather_copy(d, a, 0).start()

    full_o.wait()
    full_do.wait()
    lane = lax.broadcasted_iota(jnp.int32, (FEAT, FEAT), 1)
    aux[...] = jnp.zeros_like(aux)
    aux[:, 0:32] = lse_ref[...] * LOG2E
    stats = aux[...]
    for h in range(32):
        cols = slice(h * FEAT, (h + 1) * FEAT)
        product = o_full[:, cols].astype(F32) * do_full[:, cols].astype(F32)
        stats = jnp.where(lane == 32 + h, jnp.sum(product, axis=1, keepdims=True), stats)
    turned = stats.T
    st_own[0] = turned[0:32]
    st_own[1] = turned[32:64]
    st_send = remote(
        st_own.at[:, span(16 * yo, 16)], st_s.at[y], sem_st.at[0], sem_st.at[1], partner
    )
    st_send.start()
    st_s[y] = st_own[:, span(16 * y, 16)]

    key_row = lax.broadcasted_iota(jnp.int32, (256, 256), 0)
    query_row = lax.broadcasted_iota(jnp.int32, (256, 256), 1) % FEAT
    mask_s[0] = jnp.zeros((256, 256), F32)
    for slot in range(2):
        mask_s[1 + slot] = jnp.where(key_row > slot * FEAT + query_row, UNSEEN, 0.0)
    dq_t[...] = jnp.zeros_like(dq_t)

    own_a, own_b, before = order[2 * b], order[2 * b + 1], order[(2 * b + 31) % 32]
    query_seg = jnp.where(first_half, own_a, own_b)

    def penalty(j):
        inside = jnp.where(first_half, jnp.where(j <= z, 0.0, UNSEEN), jnp.where(own_b > own_a, 0.0, UNSEEN))
        return jnp.where(j >= 4, jnp.where(query_seg > before, 0.0, UNSEEN), inside)

    def pair_unit(a, src, s, add):
        chunks = ((z + 7 - s) % 8, (z + (s + 1) % 4) % 8)
        masked = jnp.where(jnp.logical_and(s == 3, first_half), 1 + src, 0)
        for c, j in enumerate(chunks):
            key, value = kv_s[a, j, 0], kv_s[a, j, 1]
            pen = penalty(j)
            for t in range(4):
                qr = q_s[a, src, 2 * t : 2 * t + 2].reshape(256, FEAT)
                dr = do_s[a, src, 2 * t : 2 * t + 2].reshape(256, FEAT)
                rows = [st_s[src, k, pl.ds(8 * a + 2 * t + i, 1)] for k in range(2) for i in range(2)]
                lse_row = jnp.concatenate(rows[0:2], axis=1) + pen
                delta_row = jnp.concatenate(rows[2:4], axis=1)
                x = dot(key, qr, 1, 1) * (SCALE * LOG2E) - lse_row
                if c == 1:
                    x = x - mask_s[masked]
                p = jnp.exp2(x)
                g = p * (dot(value, dr, 1, 1) - delta_row)
                ps[c, :, t * 256 : (t + 1) * 256] = p.astype(BF16)
                dss[c, :, t * 256 : (t + 1) * 256] = g.astype(BF16)
        q_all = q_s[a, src].reshape(1024, FEAT)
        do_all = do_s[a, src].reshape(1024, FEAT)
        for c, j in enumerate(chunks):
            dk = dot(dss[c], q_all, 1, 0)
            dv = dot(ps[c], do_all, 1, 0)
            if add:
                dkv[a, j, 0] += dk
                dkv[a, j, 1] += dv
            else:
                dkv[a, j, 0] = dk
                dkv[a, j, 1] = dv
        dq_t[a, src] += dot(kv_s[a, chunks[0], 0], dss[0], 0, 0) + dot(kv_s[a, chunks[1], 0], dss[1], 0, 0)

    for a in range(2):
        for t, ref in enumerate((q_s, do_s)):
            pltpu.make_async_copy(ref.at[a, y], ref.at[a, y], sem_ql.at[a, t]).wait()

    def own_step(i, carry):
        s, a = i // 2, i % 2
        for d in range(2):
            steps = jnp.where(a == d, 4, 3)

            @pl.when(s < steps)
            def _():
                gather_wait(d, a, s)

            @pl.when(s + 1 < steps)
            def _():
                gather_copy(d, a, s + 1).start()

        pair_unit(a, y, s, False)
        return carry

    lax.fori_loop(0, 8, own_step, 0)

    def reduce_copy(d, a, s):
        return remote(
            rs_out.at[d, a, s], rs_in.at[d, a, s], sem_rs.at[d, a, s], sem_rr.at[d, a, s], ring[d]
        )

    def reduce_step(d, a, s):
        left = jnp.where(a == d, 4, 3) - s
        j = (z + left) % 8 if d == 0 else (z + 8 - left) % 8

        @pl.when(s == 0)
        def _():
            rs_out[d, a, 0] = dkv[a, j].astype(BF16)

        @pl.when(s > 0)
        def _():
            before_s = jnp.maximum(s - 1, 0)
            reduce_copy(d, a, before_s).wait_recv()
            rs_out[d, a, s] = (dkv[a, j] + rs_in[d, a, before_s].astype(F32)).astype(BF16)

        reduce_copy(d, a, s).start()

    st_send.wait_recv()

    def dq_send(a):
        return remote(dq_out.at[a], dq_in.at[a], sem_dqs.at[a], sem_dqr.at[a], partner)

    def dq_cols(who, a):
        return dq_hbm.at[:, span((2 * who + a) * 1024, 1024)]

    def partner_step(i, carry):
        a, p = i // 4, i % 4

        @pl.when(p == 0)
        def _():
            for t, ref in enumerate((q_s, do_s)):
                pltpu.make_async_copy(ref.at[a, yo], ref.at[a, yo], sem_qr.at[a, t]).wait()

        pair_unit(a, yo, 3 - p, True)

        @pl.when(p == 0)
        def _():
            @pl.when(a == 0)
            def _():
                reduce_step(0, 0, jnp.int32(0))

            @pl.when(a == 1)
            def _():
                reduce_step(1, 1, jnp.int32(0))

        @pl.when(p == 1)
        def _():
            @pl.when(a == 0)
            def _():
                reduce_step(1, 0, jnp.int32(0))

            @pl.when(a == 1)
            def _():
                reduce_step(0, 1, jnp.int32(0))

        @pl.when(jnp.logical_and(a == 1, p < 3))
        def _():
            reduce_step(0, 0, p + 1)

            @pl.when(p < 2)
            def _():
                reduce_step(1, 0, p + 1)

        @pl.when(p == 3)
        def _():
            for h in range(8):
                dq_out[a, h] = (dq_t[a, yo, :, h * FEAT : (h + 1) * FEAT].T * SCALE).astype(BF16)
            dq_send(a).start()

        return carry

    lax.fori_loop(0, 8, partner_step, 0)

    for a in range(2):
        for h in range(8):
            dq_stage[0, a, :, h * FEAT : (h + 1) * FEAT] = dq_t[a, y, :, h * FEAT : (h + 1) * FEAT].T * SCALE
        pltpu.make_async_copy(dq_stage.at[0, a], dq_cols(y, a), sem_out.at[0, a]).start()

    def late_step(s, carry):
        @pl.when(s < 3)
        def _():
            reduce_step(0, 1, s)

        reduce_step(1, 1, s)
        return carry

    lax.fori_loop(1, 4, late_step, 0)

    bh = jnp.where(first_half, b, prv)

    def finish(a):
        reduce_copy(0, a, 3 - a).wait_recv()
        reduce_copy(1, a, 2 + a).wait_recv()
        for kv, (ref, factor) in enumerate(((dk_hbm, SCALE), (dv_hbm, 1.0))):
            total = dkv[a, z, kv] + rs_in[0, a, 3 - a, kv].astype(F32) + rs_in[1, a, 2 + a, kv].astype(F32)
            fin[a, kv] = total * factor
            dst = ref.at[:, span((2 * y + a) * FEAT, FEAT)]
            far = fin.at[a, kv, span(yo * FEAT, FEAT)]
            near = fin.at[a, kv, span(y * FEAT, FEAT)]
            remote(far, dst, sem_fs.at[0, a, kv], sem_fr.at[y, a, kv], (bh, 2 * z + yo)).start()

            @pl.when(first_half)
            def _():
                pltpu.make_async_copy(near, dst, sem_fr.at[y, a, kv]).start()

            @pl.when(jnp.logical_not(first_half))
            def _():
                remote(near, dst, sem_fs.at[1, a, kv], sem_fr.at[y, a, kv], (bh, hd)).start()

    finish(0)
    finish(1)

    for a in range(2):
        dq_send(a).wait_recv()
        for h in range(8):
            dq_stage[1, a, :, h * FEAT : (h + 1) * FEAT] = dq_in[a, h].astype(F32)
        pltpu.make_async_copy(dq_stage.at[1, a], dq_cols(yo, a), sem_out.at[1, a]).start()

    for a in range(2):
        for t, ref in enumerate((q_s, do_s)):
            pltpu.make_async_copy(ref.at[a, y], ref.at[a, y], sem_qs.at[a, t]).wait()
        for kv in range(2):
            half = kv_s.at[a, 0, kv, 0:FEAT]
            whole = fin.at[a, kv, 0:FEAT]
            pltpu.make_async_copy(half, half, sem_as.at[0, a, kv]).wait()
            pltpu.make_async_copy(whole, whole, sem_fs.at[0, a, kv]).wait()

            @pl.when(jnp.logical_not(first_half))
            def _():
                pltpu.make_async_copy(half, half, sem_as.at[1, a, kv]).wait()
                pltpu.make_async_copy(whole, whole, sem_fs.at[1, a, kv]).wait()

            for who in range(2):
                pltpu.make_async_copy(whole, whole, sem_fr.at[who, a, kv]).wait()
        for d in range(2):
            for s in range(4 if d == a else 3):
                gather_copy(d, a, s).wait_send()
                reduce_copy(d, a, s).wait_send()
        dq_send(a).wait_send()
        for who, device in enumerate((y, yo)):
            pltpu.make_async_copy(dq_stage.at[who, a], dq_cols(device, a), sem_out.at[who, a]).wait()
    st_send.wait_send()


def core(queries, key_matrix, value_matrix, saved_output, output_gradient, saved_logsumexp, block_order):
    dma = pltpu.SemaphoreType.DMA
    vmem = pltpu.VMEM
    anywhere = pl.BlockSpec(memory_space=pl.ANY)
    return pl.pallas_call(
        kernel,
        out_shape=[
            jax.ShapeDtypeStruct(queries.shape, F32),
            jax.ShapeDtypeStruct(key_matrix.shape, F32),
            jax.ShapeDtypeStruct(value_matrix.shape, F32),
        ],
        in_specs=[pl.BlockSpec(memory_space=pltpu.SMEM)]
        + [anywhere] * 5
        + [pl.BlockSpec(memory_space=pltpu.VMEM)],
        out_specs=[anywhere] * 3,
        scratch_shapes=[
            vmem((2, 2, 8, 128, 128), BF16),
            vmem((2, 2, 8, 128, 128), BF16),
            vmem((2, 8, 2, 256, 128), BF16),
            vmem((128, 4096), BF16),
            vmem((128, 4096), BF16),
            vmem((2, 32, 128), F32),
            vmem((2, 2, 16, 128), F32),
            vmem((128, 128), F32),
            vmem((3, 256, 256), F32),
            vmem((2, 256, 1024), BF16),
            vmem((2, 256, 1024), BF16),
            vmem((2, 2, 128, 1024), F32),
            vmem((2, 8, 2, 256, 128), F32),
            vmem((2, 2, 4, 2, 256, 128), BF16),
            vmem((2, 2, 4, 2, 256, 128), BF16),
            vmem((2, 2, 256, 128), F32),
            vmem((2, 8, 128, 128), BF16),
            vmem((2, 8, 128, 128), BF16),
            vmem((2, 2, 128, 1024), F32),
            dma((2,)),
            dma((2, 2)),
            dma((2, 2)),
            dma((2, 2)),
            dma((2,)),
            dma((2, 2, 2)),
            dma((2, 2, 2)),
            dma((2, 2, 4)),
            dma((2, 2, 4)),
            dma((2, 2, 4)),
            dma((2, 2, 4)),
            dma((2, 2, 2)),
            dma((2, 2, 2)),
            dma((2,)),
            dma((2,)),
            dma((2, 2)),
        ],
        compiler_params=pltpu.CompilerParams(
            collective_id=0, has_side_effects=True, vmem_limit_bytes=48 << 20
        ),
        name="attention_backward",
    )(
        block_order, queries, key_matrix, value_matrix, saved_output, output_gradient, saved_logsumexp
    )


def solution(mesh):
    rows = P(("blk", "head"), None)
    return jax.shard_map(
        core,
        mesh=mesh,
        in_specs=(rows,) * 6 + (P(),),
        out_specs=(rows,) * 3,
        check_vma=False,
    )
```

```python
import functools

import jax
import jax.numpy as jnp
from jax import lax
from jax.experimental import pallas as pl
from jax.experimental.pallas import tpu as pltpu
from jax.sharding import PartitionSpec as P

F32 = jnp.float32
BF16 = jnp.bfloat16
FEAT = 128
SCALE = FEAT**-0.5
LOG2E = 1.4426950408889634
UNSEEN = 1e30
MESH = pl.DeviceIdType.MESH

UNITS = (
    ((0, -1), (0, 1), False),
    ((1, -1), (1, 1), False),
    ((0, -2), (0, 2), False),
    ((1, -2), (1, 2), False),
    ((0, -1), (0, 1), True),
    ((0, -2), (0, 2), True),
    ((0, -3), (0, 3), False),
    ((0, -3), (0, 3), True),
    ((0, 4), (1, -3), False),
    ((0, 4), (0, 0), True),
    ((1, 3), (1, 4), False),
    ((1, 4), (1, 0), True),
    ((1, -3), (1, 3), True),
    ((1, -2), (1, 2), True),
    ((1, -1), (1, 1), True),
)


def dot(a, b, ca, cb):
    return lax.dot_general(a, b, (((ca,), (cb,)), ((), ())), preferred_element_type=F32)


def pick(n, values):
    out = jnp.int32(values[-1])
    for i, value in enumerate(values[:-1]):
        out = jnp.where(n == i, value, out)
    return out


def span(start, size):
    return pl.ds(pl.multiple_of(start, size), size)


def kernel(
    order_hbm, q_hbm, k_hbm, v_hbm, o_hbm, do_hbm, lse_hbm, dq_hbm, dk_hbm, dv_hbm,
    order, q_s, do_s, kv_s, o_full, do_full, lse_s, st_own, st_s, mask_s, ps, dss, dq_t, dkv,
    rs_in, rs_out, fin, dq_out, dq_in, dq_stage,
    sem_full, sem_ql, sem_qr, sem_qs, sem_st, sem_ar, sem_as, sem_gr, sem_gs, sem_rr, sem_rs,
    sem_fr, sem_fs, sem_dqr, sem_dqs, sem_out,
):
    b = lax.axis_index("blk")
    hd = lax.axis_index("head")
    z = hd // 2
    y = hd % 2
    yo = 1 - y
    partner = (b, 2 * z + yo)
    ring = ((b, (hd + 2) % 16), (b, (hd + 14) % 16))
    nxt = (b + 1) % 16
    prv = (b + 15) % 16
    first_half = z < 4
    later_half = jnp.logical_not(first_half)

    barrier = pltpu.get_barrier_semaphore()
    up, down = (hd + 2) % 16, (hd + 14) % 16
    peers = [partner, ring[0], ring[1]]
    peers += [(other, at) for other in (nxt, prv) for at in (hd, 2 * z + yo, up, down)]
    for peer in peers:
        pl.semaphore_signal(barrier, inc=1, device_id=peer, device_id_type=MESH)

    loads = [
        pltpu.make_async_copy(src, dst, sem_full.at[i])
        for i, (src, dst) in enumerate(
            ((o_hbm, o_full), (do_hbm, do_full), (lse_hbm, lse_s), (order_hbm, order))
        )
    ]
    for load in loads:
        load.start()

    def local_part(a, kv):
        ref = (k_hbm, v_hbm)[kv]
        return pltpu.make_async_copy(
            ref.at[:, span((2 * y + a) * FEAT, FEAT)], kv_s.at[a, z, y, kv], sem_ar.at[a, kv, y]
        )

    @pl.when(first_half)
    def _():
        for a in range(2):
            for kv in range(2):
                local_part(a, kv).start()

    for a in range(2):
        for t, (src, dst) in enumerate(((q_hbm, q_s), (do_hbm, do_s))):

            def one(h, c):
                pltpu.make_async_copy(
                    src.at[:, span((16 * y + 8 * a + h) * FEAT, FEAT)], dst.at[a, y, h], sem_ql.at[a, t]
                ).start()
                return c

            lax.fori_loop(0, 8, one, 0)

    dkv[...] = jnp.zeros_like(dkv)
    dq_t[...] = jnp.zeros_like(dq_t)
    key_row = lax.broadcasted_iota(jnp.int32, (256, 256), 0)
    query_row = lax.broadcasted_iota(jnp.int32, (256, 256), 1) % FEAT
    mask_s[0] = jnp.zeros((256, 256), F32)
    for slot in range(2):
        mask_s[1 + slot] = jnp.where(key_row > slot * FEAT + query_row, UNSEEN, 0.0)

    pl.semaphore_wait(barrier, len(peers))

    def remote(src, dst, ss, rs, dev):
        return pltpu.make_async_remote_copy(
            src_ref=src, dst_ref=dst, send_sem=ss, recv_sem=rs, device_id=dev, device_id_type=MESH
        )

    bt = jnp.where(first_half, b, nxt)
    for a in range(2):
        for kv, ref in enumerate((k_hbm, v_hbm)):
            near = ref.at[:, span((2 * y + a) * FEAT, FEAT)]
            dst = kv_s.at[a, z, y, kv]
            for d, at in enumerate((up, down)):
                remote(near, dst, sem_gs.at[d, a, 0, y], sem_gr.at[d, a, 0, y], (bt, at)).start()
    for a in range(2):
        for kv, ref in enumerate((k_hbm, v_hbm)):
            far = ref.at[:, span((2 * yo + a) * FEAT, FEAT)]
            remote(
                far, kv_s.at[a, z, y, kv], sem_as.at[0, a, kv], sem_ar.at[a, kv, y], (bt, 2 * z + yo)
            ).start()
    for a in range(2):
        for kv, ref in enumerate((k_hbm, v_hbm)):
            near = ref.at[:, span((2 * y + a) * FEAT, FEAT)]

            @pl.when(later_half)
            def _():
                remote(
                    near, kv_s.at[a, z, y, kv], sem_as.at[1, a, kv], sem_ar.at[a, kv, y], (bt, hd)
                ).start()

    def q_part(g):
        a, quad, t = g // 4, (g // 2) % 2, g % 2
        return a, quad, t, ((q_hbm, q_s), (do_hbm, do_s))[t]

    def q_send(g):
        a, quad, t, (src, dst) = q_part(g)

        def one(h, c):
            remote(
                src.at[:, span((16 * yo + 8 * a + h) * FEAT, FEAT)], dst.at[a, y, h],
                sem_qs.at[a, t, quad], sem_qr.at[a, t, quad], partner,
            ).start()
            return c

        lax.fori_loop(4 * quad, 4 * quad + 4, one, 0)

    def q_sent(g):
        a, quad, t, (_, dst) = q_part(g)
        place = dst.at[a, y, pl.ds(4 * quad, 4)]
        pltpu.make_async_copy(place, place, sem_qs.at[a, t, quad]).wait()

    def q_next(g):
        q_sent(g)
        q_send(g + 2)

    def gather_copy(d, a, s, half):
        j = (z + 8 - s) % 8 if d == 0 else (z + s) % 8
        piece = kv_s.at[a, j, half]
        return remote(piece, piece, sem_gs.at[d, a, s, half], sem_gr.at[d, a, s, half], ring[d])

    def own_chunk(a, half):
        for kv in range(2):
            place = kv_s.at[a, z, half, kv]
            pltpu.make_async_copy(place, place, sem_ar.at[a, kv, half]).wait()

    def gather_on(slot):
        s, a, half = slot // 4, slot % 2, (y if slot % 4 < 2 else yo)
        for d in range(2):
            steps = 4 if a == d else 3
            if s < steps:
                gather_copy(d, a, s, half).wait_recv()
            if s + 1 < steps:
                gather_copy(d, a, s + 1, half).start()

    q_send(0)
    q_send(1)

    for load in loads:
        load.wait()
    lane = lax.broadcasted_iota(jnp.int32, (FEAT, FEAT), 1)
    stats = jnp.zeros((FEAT, FEAT), F32)
    for h in range(32):
        cols = slice(h * FEAT, (h + 1) * FEAT)
        product = o_full[:, cols].astype(F32) * do_full[:, cols].astype(F32)
        stats = jnp.where(lane == h, jnp.sum(product, axis=1, keepdims=True), stats)
    st_own[0] = lse_s[...] * LOG2E
    st_own[1] = stats.T[0:32]
    st_send = remote(
        st_own.at[:, span(16 * yo, 16)], st_s.at[y], sem_st.at[0], sem_st.at[1], partner
    )
    st_send.start()
    st_s[y] = st_own[:, span(16 * y, 16)]

    for a in range(2):
        own_chunk(a, yo)
        for d in range(2):
            gather_copy(d, a, 0, yo).start()
    for a in range(2):
        own_chunk(a, y)

    own_a, own_b, before = order[2 * b], order[2 * b + 1], order[(2 * b + 31) % 32]
    query_seg = jnp.where(first_half, own_a, own_b)

    def penalty(j):
        inside = jnp.where(first_half, jnp.where(j <= z, 0.0, UNSEEN), jnp.where(own_b > own_a, 0.0, UNSEEN))
        return jnp.where(j >= 4, jnp.where(query_seg > before, 0.0, UNSEEN), inside)

    def pair_unit(src, chunks, masks):
        for c, (a, j) in enumerate(chunks):
            key = kv_s[a, j, :, 0].reshape(256, FEAT)
            value = kv_s[a, j, :, 1].reshape(256, FEAT)
            pen = penalty(j)
            for t in range(4):
                qr = q_s[a, src, 2 * t : 2 * t + 2].reshape(256, FEAT)
                dr = do_s[a, src, 2 * t : 2 * t + 2].reshape(256, FEAT)
                rows = [st_s[src, k, pl.ds(8 * a + 2 * t + i, 1)] for k in range(2) for i in range(2)]
                lse_row = jnp.concatenate(rows[0:2], axis=1) + pen
                delta_row = jnp.concatenate(rows[2:4], axis=1)
                x = dot(key, qr, 1, 1) * (SCALE * LOG2E) - lse_row
                if masks[c] is not None:
                    x = x - mask_s[masks[c]]
                p = jnp.exp2(x)
                g = p * (dot(value, dr, 1, 1) - delta_row)
                ps[c, :, t * 256 : (t + 1) * 256] = p.astype(BF16)
                dss[c, :, t * 256 : (t + 1) * 256] = g.astype(BF16)
        for c, (a, j) in enumerate(chunks):
            dkv[a, j, 0] += dot(dss[c], q_s[a, src].reshape(1024, FEAT), 1, 0)
            dkv[a, j, 1] += dot(ps[c], do_s[a, src].reshape(1024, FEAT), 1, 0)
            dq_t[a, src] += dot(kv_s[a, j, :, 0].reshape(256, FEAT), dss[c], 0, 0)

    for a in range(2):
        for t, ref in enumerate((q_s, do_s)):
            pltpu.make_async_copy(ref.at[a, y], ref.at[a, y], sem_ql.at[a, t]).wait()
    diagonal = jnp.where(first_half, 1 + y, 0)
    pair_unit(y, ((0, z), (1, z)), (diagonal, diagonal))

    def reduce_copy(d, a, s, kv):
        return remote(
            rs_out.at[d, a, s, kv], rs_in.at[d, a, s, kv], sem_rs.at[d, a, s, kv], sem_rr.at[d, a, s, kv], ring[d]
        )

    def reduce_step(d, a, s):
        left = (4 if a == d else 3) - s
        j = (z + left) % 8 if d == 0 else (z + 8 - left) % 8
        for kv in (1, 0):
            part = dkv[a, j, kv]
            if s > 0:
                reduce_copy(d, a, s - 1, kv).wait_recv()
                part = part + rs_in[d, a, s - 1, kv].astype(F32)
            rs_out[d, a, s, kv] = part.astype(BF16)
            reduce_copy(d, a, s, kv).start()

    def dq_send(a):
        return remote(dq_out.at[a], dq_in.at[a], sem_dqs.at[a], sem_dqr.at[a], partner)

    def dq_cols(who, a):
        return dq_hbm.at[:, span((2 * who + a) * 1024, 1024)]

    def dq_away(a):
        for h in range(8):
            dq_out[a, h] = (dq_t[a, yo, :, h * FEAT : (h + 1) * FEAT].T * SCALE).astype(BF16)
        dq_send(a).start()

    def dq_keep(a):
        for h in range(8):
            dq_stage[0, a, :, h * FEAT : (h + 1) * FEAT] = dq_t[a, y, :, h * FEAT : (h + 1) * FEAT].T * SCALE
        pltpu.make_async_copy(dq_stage.at[0, a], dq_cols(y, a), sem_out.at[0, a]).start()

    def dq_back(a):
        dq_send(a).wait_recv()
        for h in range(8):
            dq_stage[1, a, :, h * FEAT : (h + 1) * FEAT] = dq_in[a, h].astype(F32)
        pltpu.make_async_copy(dq_stage.at[1, a], dq_cols(yo, a), sem_out.at[1, a]).start()

    def partner_rows(a):
        for g in range(4 * a, 4 * a + 4):
            _, quad, t, (_, dst) = q_part(g)
            place = dst.at[a, yo, pl.ds(4 * quad, 4)]
            pltpu.make_async_copy(place, place, sem_qr.at[a, t, quad]).wait()

    bh = jnp.where(first_half, b, prv)

    def finish(a):
        for kv, (ref, factor) in ((1, (dv_hbm, 1.0)), (0, (dk_hbm, SCALE))):
            reduce_copy(0, a, 3 - a, kv).wait_recv()
            reduce_copy(1, a, 2 + a, kv).wait_recv()
            total = dkv[a, z, kv] + rs_in[0, a, 3 - a, kv].astype(F32) + rs_in[1, a, 2 + a, kv].astype(F32)
            fin[a, kv] = total * factor
            dst = ref.at[:, span((2 * y + a) * FEAT, FEAT)]
            far = fin.at[a, kv, span(yo * FEAT, FEAT)]
            near = fin.at[a, kv, span(y * FEAT, FEAT)]
            remote(far, dst, sem_fs.at[0, a, kv], sem_fr.at[y, a, kv], (bh, 2 * z + yo)).start()

            @pl.when(first_half)
            def _():
                pltpu.make_async_copy(near, dst, sem_fr.at[y, a, kv]).start()

            @pl.when(later_half)
            def _():
                remote(near, dst, sem_fs.at[1, a, kv], sem_fr.at[y, a, kv], (bh, hd)).start()

    before_unit = {
        0: lambda: (gather_on(0), gather_on(1), gather_on(2)),
        1: lambda: (gather_on(3), q_next(0)),
        2: lambda: (gather_on(4), q_next(1), gather_on(5), gather_on(6)),
        3: lambda: (gather_on(7), q_next(2)),
        4: lambda: (gather_on(8), q_next(3), st_send.wait_recv(), partner_rows(0)),
        5: lambda: gather_on(9),
        6: lambda: (gather_on(10), q_next(4)),
        7: lambda: gather_on(11),
        8: lambda: (q_next(5), gather_on(12), gather_on(13), gather_on(14)),
        10: lambda: gather_on(15),
        11: lambda: partner_rows(1),
    }
    after_unit = {
        7: lambda: reduce_step(1, 0, 0),
        9: lambda: (reduce_step(0, 0, 0), dq_away(0)),
        10: lambda: reduce_step(1, 0, 1),
        11: lambda: reduce_step(1, 1, 0),
        12: lambda: (reduce_step(0, 1, 0), reduce_step(0, 0, 1)),
        13: lambda: reduce_step(1, 0, 2),
        14: lambda: (dq_away(1), reduce_step(1, 1, 1), reduce_step(0, 1, 1), reduce_step(0, 0, 2)),
    }

    def unit_step(n, carry):
        for at, action in before_unit.items():
            pl.when(n == at)(lambda action=action: (action(), None)[1])
        chunks = tuple(
            (pick(n, [u[c][0] for u in UNITS]), (z + 8 + pick(n, [u[c][1] for u in UNITS])) % 8)
            for c in range(2)
        )
        away = pick(n, [int(u[2]) for u in UNITS])
        src = jnp.where(away == 1, yo, y)
        masked = jnp.where(jnp.logical_and(chunks[1][1] == z, first_half), 1 + src, 0)
        pair_unit(src, chunks, (None, masked))
        for at, action in after_unit.items():
            pl.when(n == at)(lambda action=action: (action(), None)[1])
        return carry

    lax.fori_loop(0, len(UNITS), unit_step, 0)

    dq_keep(0)
    dq_keep(1)
    reduce_step(1, 1, 2)
    reduce_step(0, 1, 2)
    reduce_step(0, 0, 3)
    dq_back(0)
    reduce_step(1, 1, 3)
    finish(0)
    dq_back(1)
    finish(1)

    q_sent(6)
    q_sent(7)
    for a in range(2):
        for kv in range(2):
            half = kv_s.at[a, 0, 0, kv]
            whole = fin.at[a, kv, 0:FEAT]
            pltpu.make_async_copy(half, half, sem_as.at[0, a, kv]).wait()
            pltpu.make_async_copy(whole, whole, sem_fs.at[0, a, kv]).wait()

            @pl.when(later_half)
            def _():
                pltpu.make_async_copy(half, half, sem_as.at[1, a, kv]).wait()
                pltpu.make_async_copy(whole, whole, sem_fs.at[1, a, kv]).wait()

            for who in range(2):
                pltpu.make_async_copy(whole, whole, sem_fr.at[who, a, kv]).wait()
        for d in range(2):
            for s in range(4 if d == a else 3):
                for i in range(2):
                    gather_copy(d, a, s, i).wait_send()
                    reduce_copy(d, a, s, i).wait_send()
        dq_send(a).wait_send()
        for who, device in enumerate((y, yo)):
            pltpu.make_async_copy(dq_stage.at[who, a], dq_cols(device, a), sem_out.at[who, a]).wait()
    st_send.wait_send()


def settle(*refs):
    sources, results, held, sems = refs[0:3], refs[3:6], refs[6:9], refs[9]
    loads, stores = [], []
    for src, mid, dst, parts in zip(sources, held, results, (8, 2, 2)):
        rows = src.shape[0] // parts
        for i in range(parts):
            at = pl.ds(i * rows, rows)
            n = len(loads)
            loads.append(pltpu.make_async_copy(src.at[at], mid.at[at], sems.at[0, n]))
            stores.append(pltpu.make_async_copy(mid.at[at], dst.at[at], sems.at[1, n]))
    for load in loads:
        load.start()
    for load, store in zip(loads, stores):
        load.wait()
        store.start()
    for store in stores:
        store.wait()


def core(queries, key_matrix, value_matrix, saved_output, output_gradient, saved_logsumexp, block_order):
    dma = pltpu.SemaphoreType.DMA
    vmem = pltpu.VMEM
    hbm = pl.BlockSpec(memory_space=pltpu.HBM)
    shapes = [
        jax.ShapeDtypeStruct(array.shape, F32) for array in (queries, key_matrix, value_matrix)
    ]
    gradients = pl.pallas_call(
        kernel,
        out_shape=shapes,
        in_specs=[hbm] * 7,
        out_specs=[hbm] * 3,
        scratch_shapes=[
            pltpu.SMEM((32,), jnp.int32),
            vmem((2, 2, 8, 128, 128), BF16),
            vmem((2, 2, 8, 128, 128), BF16),
            vmem((2, 8, 2, 2, 128, 128), BF16),
            vmem((128, 4096), BF16),
            vmem((128, 4096), BF16),
            vmem((32, 128), F32),
            vmem((2, 32, 128), F32),
            vmem((2, 2, 16, 128), F32),
            vmem((3, 256, 256), F32),
            vmem((2, 256, 1024), BF16),
            vmem((2, 256, 1024), BF16),
            vmem((2, 2, 128, 1024), F32),
            vmem((2, 8, 2, 256, 128), F32),
            vmem((2, 2, 4, 2, 256, 128), BF16),
            vmem((2, 2, 4, 2, 256, 128), BF16),
            vmem((2, 2, 256, 128), F32),
            vmem((2, 8, 128, 128), BF16),
            vmem((2, 8, 128, 128), BF16),
            vmem((2, 2, 128, 1024), F32),
            dma((4,)),
            dma((2, 2)),
            dma((2, 2, 2)),
            dma((2, 2, 2)),
            dma((2,)),
            dma((2, 2, 2)),
            dma((2, 2, 2)),
            dma((2, 2, 4, 2)),
            dma((2, 2, 4, 2)),
            dma((2, 2, 4, 2)),
            dma((2, 2, 4, 2)),
            dma((2, 2, 2)),
            dma((2, 2, 2)),
            dma((2,)),
            dma((2,)),
            dma((2, 2)),
        ],
        compiler_params=pltpu.CompilerParams(
            collective_id=0, has_side_effects=True, vmem_limit_bytes=62 << 20
        ),
        name="attention_backward",
    )(
        block_order, queries, key_matrix, value_matrix, saved_output, output_gradient, saved_logsumexp.T
    )
    return pl.pallas_call(
        settle,
        out_shape=shapes,
        in_specs=[hbm] * 3,
        out_specs=[hbm] * 3,
        scratch_shapes=[vmem(shape.shape, F32) for shape in shapes] + [dma((2, 12))],
        compiler_params=pltpu.CompilerParams(vmem_limit_bytes=62 << 20),
        name="settle",
    )(*gradients)


def solution(mesh):
    rows = P(("blk", "head"), None)
    return jax.shard_map(
        core,
        mesh=mesh,
        in_specs=(rows,) * 6 + (P(),),
        out_specs=(rows,) * 3,
        check_vma=False,
    )
```

```python
import functools

import jax
import jax.numpy as jnp
from jax import lax
from jax.experimental import pallas as pl
from jax.experimental.pallas import tpu as pltpu
from jax.sharding import PartitionSpec as P

F32 = jnp.float32
BF16 = jnp.bfloat16
FEAT = 128
SCALE = FEAT**-0.5
LOG2E = 1.4426950408889634
UNSEEN = 1e30
MESH = pl.DeviceIdType.MESH

UNITS = (
    ((0, -1), (0, 1), False),
    ((1, -1), (1, 1), False),
    ((0, -2), (0, 2), False),
    ((1, -2), (1, 2), False),
    ((0, -1), (0, 1), True),
    ((0, -2), (0, 2), True),
    ((0, -3), (0, 3), False),
    ((0, -3), (0, 3), True),
    ((0, 4), (1, -3), False),
    ((0, 4), (0, 0), True),
    ((1, 3), (1, 4), False),
    ((1, 4), (1, 0), True),
    ((1, -3), (1, 3), True),
    ((1, -2), (1, 2), True),
    ((1, -1), (1, 1), True),
)


def dot(a, b, ca, cb):
    return lax.dot_general(a, b, (((ca,), (cb,)), ((), ())), preferred_element_type=F32)


def pick(n, values):
    out = jnp.int32(values[-1])
    for i, value in enumerate(values[:-1]):
        out = jnp.where(n == i, value, out)
    return out


def span(start, size):
    return pl.ds(pl.multiple_of(start, size), size)


def kernel(
    order_hbm, q_hbm, k_hbm, v_hbm, o_hbm, do_hbm, lse_hbm, dq_hbm, dk_hbm, dv_hbm,
    order, q_s, do_s, kv_s, o_full, do_full, lse_s, st_own, st_s, mask_s, ps, dss, dq_t, dkv,
    rs_in, rs_out, own_out, home_in, fin, dq_out, dq_in, dq_stage,
    sem_full, sem_ql, sem_qr, sem_qs, sem_st, sem_ar, sem_as, sem_gr, sem_gs, sem_rr, sem_rs,
    sem_hr, sem_hs, sem_os, sem_fin, sem_dqr, sem_dqs, sem_out,
):
    b = lax.axis_index("blk")
    hd = lax.axis_index("head")
    z = hd // 2
    y = hd % 2
    yo = 1 - y
    partner = (b, 2 * z + yo)
    ring = ((b, (hd + 2) % 16), (b, (hd + 14) % 16))
    nxt = (b + 1) % 16
    prv = (b + 15) % 16
    first_half = z < 4
    later_half = jnp.logical_not(first_half)

    barrier = pltpu.get_barrier_semaphore()
    up, down = (hd + 2) % 16, (hd + 14) % 16
    turn = yo - y
    around = (2 * z + yo, up, down, up + turn, down + turn)
    peers = [(b, at) for at in around]
    peers += [(other, at) for other in (nxt, prv) for at in (hd,) + around]
    for peer in peers:
        pl.semaphore_signal(barrier, inc=1, device_id=peer, device_id_type=MESH)

    pl.semaphore_wait(barrier, len(peers))

    def remote(src, dst, ss, rs, dev):
        return pltpu.make_async_remote_copy(
            src_ref=src, dst_ref=dst, send_sem=ss, recv_sem=rs, device_id=dev, device_id_type=MESH
        )

    bt = jnp.where(first_half, b, nxt)
    for a in range(2):
        for kv, ref in enumerate((k_hbm, v_hbm)):
            near = ref.at[:, span((2 * y + a) * FEAT, FEAT)]
            dst = kv_s.at[a, z, y, kv]
            for d, at in enumerate((up, down)):
                remote(near, dst, sem_gs.at[d, a, 0, y], sem_gr.at[d, a, 0, y], (bt, at)).start()
    for a in range(2):
        for kv, ref in enumerate((k_hbm, v_hbm)):
            far = ref.at[:, span((2 * yo + a) * FEAT, FEAT)]
            remote(
                far, kv_s.at[a, z, y, kv], sem_as.at[0, a, kv], sem_ar.at[a, kv, y], (bt, 2 * z + yo)
            ).start()
    for a in range(2):
        for kv, ref in enumerate((k_hbm, v_hbm)):
            near = ref.at[:, span((2 * y + a) * FEAT, FEAT)]

            @pl.when(later_half)
            def _():
                remote(
                    near, kv_s.at[a, z, y, kv], sem_as.at[1, a, kv], sem_ar.at[a, kv, y], (bt, hd)
                ).start()

    def q_part(g):
        a, quad, t = g // 4, (g // 2) % 2, g % 2
        return a, quad, t, ((q_hbm, q_s), (do_hbm, do_s))[t]

    def q_send(g):
        a, quad, t, (src, dst) = q_part(g)

        def one(h, c):
            remote(
                src.at[:, span((16 * yo + 8 * a + h) * FEAT, FEAT)], dst.at[a, y, h],
                sem_qs.at[a, t, quad], sem_qr.at[a, t, quad], partner,
            ).start()
            return c

        lax.fori_loop(4 * quad, 4 * quad + 4, one, 0)

    def q_sent(g):
        a, quad, t, (_, dst) = q_part(g)
        place = dst.at[a, y, pl.ds(4 * quad, 4)]
        pltpu.make_async_copy(place, place, sem_qs.at[a, t, quad]).wait()

    def q_next(g):
        q_sent(g)
        q_send(g + 2)

    def gather_copy(d, a, s, half):
        j = (z + 8 - s) % 8 if d == 0 else (z + s) % 8
        piece = kv_s.at[a, j, half]
        return remote(piece, piece, sem_gs.at[d, a, s, half], sem_gr.at[d, a, s, half], ring[d])

    def own_chunk(a, half):
        for kv in range(2):
            place = kv_s.at[a, z, half, kv]
            pltpu.make_async_copy(place, place, sem_ar.at[a, kv, half]).wait()

    def gather_on(slot):
        s, a, half = slot // 4, slot % 2, (y if slot % 4 < 2 else yo)
        for d in range(2):
            steps = 4 if a == d else 3
            if s < steps:
                gather_copy(d, a, s, half).wait_recv()
            if s + 1 < steps:
                gather_copy(d, a, s + 1, half).start()

    q_send(0)
    q_send(1)

    loads = [
        pltpu.make_async_copy(src, dst, sem_full.at[i])
        for i, (src, dst) in enumerate(
            ((o_hbm, o_full), (do_hbm, do_full), (lse_hbm, lse_s), (order_hbm, order))
        )
    ]
    for load in loads:
        load.start()

    def local_part(a, kv):
        ref = (k_hbm, v_hbm)[kv]
        return pltpu.make_async_copy(
            ref.at[:, span((2 * y + a) * FEAT, FEAT)], kv_s.at[a, z, y, kv], sem_ar.at[a, kv, y]
        )

    @pl.when(first_half)
    def _():
        for a in range(2):
            for kv in range(2):
                local_part(a, kv).start()

    for a in range(2):
        for t, (src, dst) in enumerate(((q_hbm, q_s), (do_hbm, do_s))):

            def one(h, c):
                pltpu.make_async_copy(
                    src.at[:, span((16 * y + 8 * a + h) * FEAT, FEAT)], dst.at[a, y, h], sem_ql.at[a, t]
                ).start()
                return c

            lax.fori_loop(0, 8, one, 0)

    dkv[...] = jnp.zeros_like(dkv)
    dq_t[...] = jnp.zeros_like(dq_t)
    key_row = lax.broadcasted_iota(jnp.int32, (256, 256), 0)
    query_row = lax.broadcasted_iota(jnp.int32, (256, 256), 1) % FEAT
    mask_s[0] = jnp.zeros((256, 256), F32)
    for slot in range(2):
        mask_s[1 + slot] = jnp.where(key_row > slot * FEAT + query_row, UNSEEN, 0.0)

    for load in loads:
        load.wait()
    lane = lax.broadcasted_iota(jnp.int32, (FEAT, FEAT), 1)
    stats = jnp.zeros((FEAT, FEAT), F32)
    for h in range(32):
        cols = slice(h * FEAT, (h + 1) * FEAT)
        product = o_full[:, cols].astype(F32) * do_full[:, cols].astype(F32)
        stats = jnp.where(lane == h, jnp.sum(product, axis=1, keepdims=True), stats)
    st_own[0] = lse_s[...] * LOG2E
    st_own[1] = stats.T[0:32]
    st_send = remote(
        st_own.at[:, span(16 * yo, 16)], st_s.at[y], sem_st.at[0], sem_st.at[1], partner
    )
    st_send.start()
    st_s[y] = st_own[:, span(16 * y, 16)]

    for a in range(2):
        own_chunk(a, yo)
        for d in range(2):
            gather_copy(d, a, 0, yo).start()
    for a in range(2):
        own_chunk(a, y)

    own_a, own_b, before = order[2 * b], order[2 * b + 1], order[(2 * b + 31) % 32]
    query_seg = jnp.where(first_half, own_a, own_b)

    def penalty(j):
        inside = jnp.where(first_half, jnp.where(j <= z, 0.0, UNSEEN), jnp.where(own_b > own_a, 0.0, UNSEEN))
        return jnp.where(j >= 4, jnp.where(query_seg > before, 0.0, UNSEEN), inside)

    def pair_unit(src, chunks, masks):
        for c, (a, j) in enumerate(chunks):
            key = kv_s[a, j, :, 0].reshape(256, FEAT)
            value = kv_s[a, j, :, 1].reshape(256, FEAT)
            pen = penalty(j)
            for t in range(4):
                qr = q_s[a, src, 2 * t : 2 * t + 2].reshape(256, FEAT)
                dr = do_s[a, src, 2 * t : 2 * t + 2].reshape(256, FEAT)
                rows = [st_s[src, k, pl.ds(8 * a + 2 * t + i, 1)] for k in range(2) for i in range(2)]
                lse_row = jnp.concatenate(rows[0:2], axis=1) + pen
                delta_row = jnp.concatenate(rows[2:4], axis=1)
                x = dot(key, qr, 1, 1) * (SCALE * LOG2E) - lse_row
                if masks[c] is not None:
                    x = x - mask_s[masks[c]]
                p = jnp.exp2(x)
                g = p * (dot(value, dr, 1, 1) - delta_row)
                ps[c, :, t * 256 : (t + 1) * 256] = p.astype(BF16)
                dss[c, :, t * 256 : (t + 1) * 256] = g.astype(BF16)
        for c, (a, j) in enumerate(chunks):
            dkv[a, j, 0] += dot(dss[c], q_s[a, src].reshape(1024, FEAT), 1, 0)
            dkv[a, j, 1] += dot(ps[c], do_s[a, src].reshape(1024, FEAT), 1, 0)
            dq_t[a, src] += dot(kv_s[a, j, :, 0].reshape(256, FEAT), dss[c], 0, 0)

    for a in range(2):
        for t, ref in enumerate((q_s, do_s)):
            pltpu.make_async_copy(ref.at[a, y], ref.at[a, y], sem_ql.at[a, t]).wait()
    diagonal = jnp.where(first_half, 1 + y, 0)
    pair_unit(y, ((0, z), (1, z)), (diagonal, diagonal))

    def reduce_copy(d, a, s, kv):
        return remote(
            rs_out.at[d, a, s, kv], rs_in.at[d, a, s, kv], sem_rs.at[d, a, s, kv], sem_rr.at[d, a, s, kv], ring[d]
        )

    def home_copy(d, a, kv, half):
        to_z = (z + 1) % 8 if d == 0 else (z + 7) % 8
        device = (jnp.where(to_z < 4, b, prv), 2 * to_z + half)
        return remote(
            rs_out.at[d, a, 3 if d == a else 2, kv, half], home_in.at[y, d, a, kv],
            sem_hs.at[d, a, kv, half], sem_hr.at[y, d, a, kv], device,
        )

    def reduce_step(d, a, s):
        steps = 4 if a == d else 3
        left = steps - s
        j = (z + left) % 8 if d == 0 else (z + 8 - left) % 8
        for kv in (1, 0):
            part = dkv[a, j, kv].reshape(2, FEAT, FEAT)
            if s > 0:
                reduce_copy(d, a, s - 1, kv).wait_recv()
                part = part + rs_in[d, a, s - 1, kv].astype(F32)
            rs_out[d, a, s, kv] = part.astype(BF16)
            if left > 1:
                reduce_copy(d, a, s, kv).start()
            else:
                for half in range(2):
                    home_copy(d, a, kv, half).start()

    def own_copy(a, kv, half, device):
        return remote(
            own_out.at[a, kv, half], home_in.at[y, 2, a, kv], sem_os.at[a, kv, half], sem_hr.at[y, 2, a, kv], device
        )

    def own_send(a):
        for kv in range(2):
            for half in range(2):
                own_out[a, kv, half] = dkv[a, z, kv, half * FEAT : (half + 1) * FEAT].astype(BF16)

            @pl.when(first_half)
            def _():
                own_copy(a, kv, yo, (b, 2 * z + yo)).start()

            @pl.when(later_half)
            def _():
                for half in range(2):
                    own_copy(a, kv, half, (prv, 2 * z + half)).start()

    def dq_send(a):
        return remote(dq_out.at[a], dq_in.at[a], sem_dqs.at[a], sem_dqr.at[a], partner)

    def dq_cols(who, a):
        return dq_hbm.at[:, span((2 * who + a) * 1024, 1024)]

    def dq_away(a):
        for h in range(8):
            dq_out[a, h] = (dq_t[a, yo, :, h * FEAT : (h + 1) * FEAT].T * SCALE).astype(BF16)
        dq_send(a).start()

    def dq_keep(a):
        for h in range(8):
            dq_stage[0, a, :, h * FEAT : (h + 1) * FEAT] = dq_t[a, y, :, h * FEAT : (h + 1) * FEAT].T * SCALE
        pltpu.make_async_copy(dq_stage.at[0, a], dq_cols(y, a), sem_out.at[0, a]).start()

    def dq_back(a):
        dq_send(a).wait_recv()
        for h in range(8):
            dq_stage[1, a, :, h * FEAT : (h + 1) * FEAT] = dq_in[a, h].astype(F32)
        pltpu.make_async_copy(dq_stage.at[1, a], dq_cols(yo, a), sem_out.at[1, a]).start()

    def partner_rows(a):
        for g in range(4 * a, 4 * a + 4):
            _, quad, t, (_, dst) = q_part(g)
            place = dst.at[a, yo, pl.ds(4 * quad, 4)]
            pltpu.make_async_copy(place, place, sem_qr.at[a, t, quad]).wait()

    def landed(pair, part, a, kv):
        place = home_in.at[pair, part, a, kv]
        pltpu.make_async_copy(place, place, sem_hr.at[pair, part, a, kv]).wait()
        return home_in[pair, part, a, kv].astype(F32)

    def finish(a):
        for kv, (ref, factor) in ((1, (dv_hbm, 1.0)), (0, (dk_hbm, SCALE))):
            for who, pair in enumerate((y, yo)):
                total = landed(pair, 0, a, kv) + landed(pair, 1, a, kv)
                mine = first_half if who == 0 else False

                @pl.when(mine)
                def _():
                    fin[who, a, kv] = (total + dkv[a, z, kv, span(y * FEAT, FEAT)]) * factor

                @pl.when(jnp.logical_not(mine))
                def _():
                    fin[who, a, kv] = (total + landed(pair, 2, a, kv)) * factor

                pltpu.make_async_copy(
                    fin.at[who, a, kv], ref.at[:, span((2 * pair + a) * FEAT, FEAT)], sem_fin.at[who, a, kv]
                ).start()

    before_unit = {
        0: lambda: (gather_on(0), gather_on(1), gather_on(2)),
        1: lambda: (gather_on(3), q_next(0)),
        2: lambda: (gather_on(4), q_next(1), gather_on(5), gather_on(6)),
        3: lambda: (gather_on(7), q_next(2)),
        4: lambda: (gather_on(8), q_next(3), st_send.wait_recv(), partner_rows(0)),
        5: lambda: gather_on(9),
        6: lambda: (gather_on(10), q_next(4)),
        7: lambda: gather_on(11),
        8: lambda: (q_next(5), gather_on(12), gather_on(13), gather_on(14)),
        10: lambda: gather_on(15),
        11: lambda: partner_rows(1),
    }
    after_unit = {
        7: lambda: reduce_step(1, 0, 0),
        9: lambda: (reduce_step(0, 0, 0), dq_away(0), own_send(0)),
        10: lambda: (reduce_step(1, 0, 1), dq_keep(0), dq_keep(1)),
        11: lambda: (reduce_step(1, 1, 0), reduce_step(0, 0, 1), own_send(1)),
        12: lambda: (reduce_step(0, 1, 0), reduce_step(1, 0, 2)),
        13: lambda: (reduce_step(1, 1, 1), reduce_step(0, 0, 2)),
        14: lambda: (reduce_step(0, 1, 1), dq_away(1), reduce_step(1, 1, 2), reduce_step(0, 0, 3)),
    }

    def unit_step(n, carry):
        for at, action in before_unit.items():
            pl.when(n == at)(lambda action=action: (action(), None)[1])
        chunks = tuple(
            (pick(n, [u[c][0] for u in UNITS]), (z + 8 + pick(n, [u[c][1] for u in UNITS])) % 8)
            for c in range(2)
        )
        away = pick(n, [int(u[2]) for u in UNITS])
        src = jnp.where(away == 1, yo, y)
        masked = jnp.where(jnp.logical_and(chunks[1][1] == z, first_half), 1 + src, 0)
        pair_unit(src, chunks, (None, masked))
        for at, action in after_unit.items():
            pl.when(n == at)(lambda action=action: (action(), None)[1])
        return carry

    lax.fori_loop(0, len(UNITS), unit_step, 0)

    reduce_step(0, 1, 2)
    reduce_step(1, 1, 3)
    dq_back(0)
    finish(0)
    dq_back(1)
    finish(1)

    q_sent(6)
    q_sent(7)
    for a in range(2):
        for kv in range(2):
            place = kv_s.at[a, 0, 0, kv]
            pltpu.make_async_copy(place, place, sem_as.at[0, a, kv]).wait()

            @pl.when(first_half)
            def _():
                own_copy(a, kv, yo, partner).wait_send()

            @pl.when(later_half)
            def _():
                pltpu.make_async_copy(place, place, sem_as.at[1, a, kv]).wait()
                for half in range(2):
                    own_copy(a, kv, half, partner).wait_send()

            for who in range(2):
                pltpu.make_async_copy(fin.at[who, a, kv], fin.at[who, a, kv], sem_fin.at[who, a, kv]).wait()
        for d in range(2):
            steps = 4 if d == a else 3
            for half in range(2):
                for s in range(steps):
                    gather_copy(d, a, s, half).wait_send()
                for kv in range(2):
                    home_copy(d, a, kv, half).wait_send()
            for kv in range(2):
                for s in range(steps - 1):
                    reduce_copy(d, a, s, kv).wait_send()
        dq_send(a).wait_send()
        for who, device in enumerate((y, yo)):
            pltpu.make_async_copy(dq_stage.at[who, a], dq_cols(device, a), sem_out.at[who, a]).wait()
    st_send.wait_send()


def settle(*refs):
    sources, results, held, sems = refs[0:3], refs[3:6], refs[6:9], refs[9]
    loads, stores = [], []
    for src, mid, dst, parts in zip(sources, held, results, (8, 2, 2)):
        rows = src.shape[0] // parts
        for i in range(parts):
            at = pl.ds(i * rows, rows)
            n = len(loads)
            loads.append(pltpu.make_async_copy(src.at[at], mid.at[at], sems.at[0, n]))
            stores.append(pltpu.make_async_copy(mid.at[at], dst.at[at], sems.at[1, n]))
    for load in loads:
        load.start()
    for load, store in zip(loads, stores):
        load.wait()
        store.start()
    for store in stores:
        store.wait()


def core(queries, key_matrix, value_matrix, saved_output, output_gradient, saved_logsumexp, block_order):
    dma = pltpu.SemaphoreType.DMA
    vmem = pltpu.VMEM
    hbm = pl.BlockSpec(memory_space=pltpu.HBM)
    shapes = [
        jax.ShapeDtypeStruct(array.shape, F32) for array in (queries, key_matrix, value_matrix)
    ]
    gradients = pl.pallas_call(
        kernel,
        out_shape=shapes,
        in_specs=[hbm] * 7,
        out_specs=[hbm] * 3,
        scratch_shapes=[
            pltpu.SMEM((32,), jnp.int32),
            vmem((2, 2, 8, 128, 128), BF16),
            vmem((2, 2, 8, 128, 128), BF16),
            vmem((2, 8, 2, 2, 128, 128), BF16),
            vmem((128, 4096), BF16),
            vmem((128, 4096), BF16),
            vmem((32, 128), F32),
            vmem((2, 32, 128), F32),
            vmem((2, 2, 16, 128), F32),
            vmem((3, 256, 256), F32),
            vmem((2, 256, 1024), BF16),
            vmem((2, 256, 1024), BF16),
            vmem((2, 2, 128, 1024), F32),
            vmem((2, 8, 2, 256, 128), F32),
            vmem((2, 2, 3, 2, 2, 128, 128), BF16),
            vmem((2, 2, 4, 2, 2, 128, 128), BF16),
            vmem((2, 2, 2, 128, 128), BF16),
            vmem((2, 3, 2, 2, 128, 128), BF16),
            vmem((2, 2, 2, 128, 128), F32),
            vmem((2, 8, 128, 128), BF16),
            vmem((2, 8, 128, 128), BF16),
            vmem((2, 2, 128, 1024), F32),
            dma((4,)),
            dma((2, 2)),
            dma((2, 2, 2)),
            dma((2, 2, 2)),
            dma((2,)),
            dma((2, 2, 2)),
            dma((2, 2, 2)),
            dma((2, 2, 4, 2)),
            dma((2, 2, 4, 2)),
            dma((2, 2, 3, 2)),
            dma((2, 2, 3, 2)),
            dma((2, 3, 2, 2)),
            dma((2, 2, 2, 2)),
            dma((2, 2, 2)),
            dma((2, 2, 2)),
            dma((2,)),
            dma((2,)),
            dma((2, 2)),
        ],
        compiler_params=pltpu.CompilerParams(
            collective_id=0, has_side_effects=True, vmem_limit_bytes=62 << 20
        ),
        name="attention_backward",
    )(
        block_order, queries, key_matrix, value_matrix, saved_output, output_gradient, saved_logsumexp.T
    )
    return pl.pallas_call(
        settle,
        out_shape=shapes,
        in_specs=[hbm] * 3,
        out_specs=[hbm] * 3,
        scratch_shapes=[vmem(shape.shape, F32) for shape in shapes] + [dma((2, 12))],
        compiler_params=pltpu.CompilerParams(vmem_limit_bytes=62 << 20),
        name="settle",
    )(*gradients)


def solution(mesh):
    rows = P(("blk", "head"), None)
    return jax.shard_map(
        core,
        mesh=mesh,
        in_specs=(rows,) * 6 + (P(),),
        out_specs=(rows,) * 3,
        check_vma=False,
    )
```

```python
import functools

import jax
import jax.numpy as jnp
from jax import lax
from jax.experimental import pallas as pl
from jax.experimental.pallas import tpu as pltpu
from jax.sharding import PartitionSpec as P

F32 = jnp.float32
BF16 = jnp.bfloat16
FEAT = 128
SCALE = FEAT**-0.5
LOG2E = 1.4426950408889634
UNSEEN = 1e30
MESH = pl.DeviceIdType.MESH

UNITS = (
    ((0, -1), (0, 1), False),
    ((1, -1), (1, 1), False),
    ((0, -2), (0, 2), False),
    ((1, -2), (1, 2), False),
    ((0, -1), (0, 1), True),
    ((0, -2), (0, 2), True),
    ((0, -3), (0, 3), False),
    ((0, -3), (0, 3), True),
    ((0, 4), (1, -3), False),
    ((0, 4), (0, 0), True),
    ((1, 3), (1, 4), False),
    ((1, 4), (1, 0), True),
    ((1, -3), (1, 3), True),
    ((1, -2), (1, 2), True),
    ((1, -1), (1, 1), True),
)


def dot(a, b, ca, cb):
    return lax.dot_general(a, b, (((ca,), (cb,)), ((), ())), preferred_element_type=F32)


def pick(n, values):
    out = jnp.int32(values[-1])
    for i, value in enumerate(values[:-1]):
        out = jnp.where(n == i, value, out)
    return out


def span(start, size):
    return pl.ds(pl.multiple_of(start, size), size)


def kernel(
    order_hbm, q_hbm, k_hbm, v_hbm, o_hbm, do_hbm, lse_hbm, dq_hbm, dk_hbm, dv_hbm,
    order, q_s, do_s, kv_s, o_full, do_full, lse_s, st_own, st_s, mask_s, ps, dss, dq_t, dkv,
    rs_in, rs_out, own_out, home_in, fin, dq_out, dq_in, dq_stage,
    sem_full, sem_ql, sem_qr, sem_qs, sem_st, sem_ar, sem_as, sem_gr, sem_gs, sem_rr, sem_rs,
    sem_hr, sem_hs, sem_os, sem_fin, sem_dqr, sem_dqs, sem_out,
):
    b = lax.axis_index("blk")
    hd = lax.axis_index("head")
    z = hd // 2
    y = hd % 2
    yo = 1 - y
    partner = (b, 2 * z + yo)
    ring = ((b, (hd + 2) % 16), (b, (hd + 14) % 16))
    nxt = (b + 1) % 16
    prv = (b + 15) % 16
    first_half = z < 4
    later_half = jnp.logical_not(first_half)

    barrier = pltpu.get_barrier_semaphore()
    up, down = (hd + 2) % 16, (hd + 14) % 16
    turn = yo - y
    around = (2 * z + yo, up, down, up + turn, down + turn)
    peers = [(b, at) for at in around]
    peers += [(other, at) for other in (nxt, prv) for at in (hd,) + around]
    for peer in reversed(peers):
        pl.semaphore_signal(barrier, inc=1, device_id=peer, device_id_type=MESH)

    pl.semaphore_wait(barrier, len(peers))

    def remote(src, dst, ss, rs, dev):
        return pltpu.make_async_remote_copy(
            src_ref=src, dst_ref=dst, send_sem=ss, recv_sem=rs, device_id=dev, device_id_type=MESH
        )

    bt = jnp.where(first_half, b, nxt)
    for a in range(2):
        for kv, ref in enumerate((k_hbm, v_hbm)):
            near = ref.at[:, span((2 * y + a) * FEAT, FEAT)]
            dst = kv_s.at[a, z, y, kv]
            for d, at in enumerate((up, down)):
                remote(near, dst, sem_gs.at[d, a, 0, y], sem_gr.at[d, a, 0, y], (bt, at)).start()
    for a in range(2):
        for kv, ref in enumerate((k_hbm, v_hbm)):
            far = ref.at[:, span((2 * yo + a) * FEAT, FEAT)]
            remote(
                far, kv_s.at[a, z, y, kv], sem_as.at[0, a, kv], sem_ar.at[a, kv, y], (bt, 2 * z + yo)
            ).start()
    for a in range(2):
        for kv, ref in enumerate((k_hbm, v_hbm)):
            near = ref.at[:, span((2 * y + a) * FEAT, FEAT)]

            @pl.when(later_half)
            def _():
                remote(
                    near, kv_s.at[a, z, y, kv], sem_as.at[1, a, kv], sem_ar.at[a, kv, y], (bt, hd)
                ).start()

    def q_part(g):
        a, quad, t = g // 4, (g // 2) % 2, g % 2
        return a, quad, t, ((q_hbm, q_s), (do_hbm, do_s))[t]

    def q_send(g):
        a, quad, t, (src, dst) = q_part(g)

        def one(h, c):
            remote(
                src.at[:, span((16 * yo + 8 * a + h) * FEAT, FEAT)], dst.at[a, y, h],
                sem_qs.at[a, t, quad], sem_qr.at[a, t, quad], partner,
            ).start()
            return c

        lax.fori_loop(4 * quad, 4 * quad + 4, one, 0)

    def q_sent(g):
        a, quad, t, (_, dst) = q_part(g)
        place = dst.at[a, y, pl.ds(4 * quad, 4)]
        pltpu.make_async_copy(place, place, sem_qs.at[a, t, quad]).wait()

    def q_next(g):
        q_sent(g)
        q_send(g + 2)

    def gather_copy(d, a, s, half):
        j = (z + 8 - s) % 8 if d == 0 else (z + s) % 8
        piece = kv_s.at[a, j, half]
        return remote(piece, piece, sem_gs.at[d, a, s, half], sem_gr.at[d, a, s, half], ring[d])

    def own_chunk(a, half):
        for kv in range(2):
            place = kv_s.at[a, z, half, kv]
            pltpu.make_async_copy(place, place, sem_ar.at[a, kv, half]).wait()

    def gather_on(slot):
        s, a, half = slot // 4, slot % 2, (y if slot % 4 < 2 else yo)
        for d in range(2):
            steps = 4 if a == d else 3
            if s < steps:
                gather_copy(d, a, s, half).wait_recv()
            if s + 1 < steps:
                gather_copy(d, a, s + 1, half).start()

    q_send(0)
    q_send(1)

    loads = [
        pltpu.make_async_copy(src, dst, sem_full.at[i])
        for i, (src, dst) in enumerate(
            ((o_hbm, o_full), (do_hbm, do_full), (lse_hbm, lse_s), (order_hbm, order))
        )
    ]
    for load in loads:
        load.start()

    def local_part(a, kv):
        ref = (k_hbm, v_hbm)[kv]
        return pltpu.make_async_copy(
            ref.at[:, span((2 * y + a) * FEAT, FEAT)], kv_s.at[a, z, y, kv], sem_ar.at[a, kv, y]
        )

    @pl.when(first_half)
    def _():
        for a in range(2):
            for kv in range(2):
                local_part(a, kv).start()

    for a in range(2):
        for t, (src, dst) in enumerate(((q_hbm, q_s), (do_hbm, do_s))):

            def one(h, c):
                pltpu.make_async_copy(
                    src.at[:, span((16 * y + 8 * a + h) * FEAT, FEAT)], dst.at[a, y, h], sem_ql.at[a, t]
                ).start()
                return c

            lax.fori_loop(0, 8, one, 0)

    dkv[...] = jnp.zeros_like(dkv)
    dq_t[...] = jnp.zeros_like(dq_t)
    key_row = lax.broadcasted_iota(jnp.int32, (256, 256), 0)
    query_row = lax.broadcasted_iota(jnp.int32, (256, 256), 1) % FEAT
    mask_s[0] = jnp.zeros((256, 256), F32)
    for slot in range(2):
        mask_s[1 + slot] = jnp.where(key_row > slot * FEAT + query_row, UNSEEN, 0.0)

    for load in loads:
        load.wait()
    lane = lax.broadcasted_iota(jnp.int32, (FEAT, FEAT), 1)
    stats = jnp.zeros((FEAT, FEAT), F32)
    for h in range(32):
        cols = slice(h * FEAT, (h + 1) * FEAT)
        product = o_full[:, cols].astype(F32) * do_full[:, cols].astype(F32)
        stats = jnp.where(lane == h, jnp.sum(product, axis=1, keepdims=True), stats)
    st_own[0] = lse_s[...] * LOG2E
    st_own[1] = stats.T[0:32]
    st_send = remote(
        st_own.at[:, span(16 * yo, 16)], st_s.at[y], sem_st.at[0], sem_st.at[1], partner
    )
    st_send.start()
    st_s[y] = st_own[:, span(16 * y, 16)]

    for a in range(2):
        own_chunk(a, yo)
        for d in range(2):
            gather_copy(d, a, 0, yo).start()
    for a in range(2):
        own_chunk(a, y)

    own_a, own_b, before = order[2 * b], order[2 * b + 1], order[(2 * b + 31) % 32]
    query_seg = jnp.where(first_half, own_a, own_b)

    def penalty(j):
        inside = jnp.where(first_half, jnp.where(j <= z, 0.0, UNSEEN), jnp.where(own_b > own_a, 0.0, UNSEEN))
        return jnp.where(j >= 4, jnp.where(query_seg > before, 0.0, UNSEEN), inside)

    def pair_unit(src, chunks, masks):
        for c, (a, j) in enumerate(chunks):
            key = kv_s[a, j, :, 0].reshape(256, FEAT)
            value = kv_s[a, j, :, 1].reshape(256, FEAT)
            pen = penalty(j)
            for t in range(4):
                qr = q_s[a, src, 2 * t : 2 * t + 2].reshape(256, FEAT)
                dr = do_s[a, src, 2 * t : 2 * t + 2].reshape(256, FEAT)
                rows = [st_s[src, k, pl.ds(8 * a + 2 * t + i, 1)] for k in range(2) for i in range(2)]
                lse_row = jnp.concatenate(rows[0:2], axis=1) + pen
                delta_row = jnp.concatenate(rows[2:4], axis=1)
                x = dot(key, qr, 1, 1) * (SCALE * LOG2E) - lse_row
                if masks[c] is not None:
                    x = x - mask_s[masks[c]]
                p = jnp.exp2(x)
                g = p * (dot(value, dr, 1, 1) - delta_row)
                ps[c, :, t * 256 : (t + 1) * 256] = p.astype(BF16)
                dss[c, :, t * 256 : (t + 1) * 256] = g.astype(BF16)
        for c, (a, j) in enumerate(chunks):
            dkv[a, j, 0] += dot(dss[c], q_s[a, src].reshape(1024, FEAT), 1, 0)
            dkv[a, j, 1] += dot(ps[c], do_s[a, src].reshape(1024, FEAT), 1, 0)
            dq_t[a, src] += dot(kv_s[a, j, :, 0].reshape(256, FEAT), dss[c], 0, 0)

    for a in range(2):
        for t, ref in enumerate((q_s, do_s)):
            pltpu.make_async_copy(ref.at[a, y], ref.at[a, y], sem_ql.at[a, t]).wait()
    diagonal = jnp.where(first_half, 1 + y, 0)
    pair_unit(y, ((0, z), (1, z)), (diagonal, diagonal))

    def reduce_copy(d, a, s, kv):
        return remote(
            rs_out.at[d, a, s, kv], rs_in.at[d, a, s, kv], sem_rs.at[d, a, s, kv], sem_rr.at[d, a, s, kv], ring[d]
        )

    def home_copy(d, a, kv, half):
        to_z = (z + 1) % 8 if d == 0 else (z + 7) % 8
        device = (jnp.where(to_z < 4, b, prv), 2 * to_z + half)
        return remote(
            rs_out.at[d, a, 3 if d == a else 2, kv, half], home_in.at[y, d, a, kv],
            sem_hs.at[d, a, kv, half], sem_hr.at[y, d, a, kv], device,
        )

    def reduce_step(d, a, s):
        steps = 4 if a == d else 3
        left = steps - s
        j = (z + left) % 8 if d == 0 else (z + 8 - left) % 8
        for kv in (1, 0):
            part = dkv[a, j, kv].reshape(2, FEAT, FEAT)
            if s > 0:
                reduce_copy(d, a, s - 1, kv).wait_recv()
                part = part + rs_in[d, a, s - 1, kv].astype(F32)
            rs_out[d, a, s, kv] = part.astype(BF16)
            if left > 1:
                reduce_copy(d, a, s, kv).start()
            else:
                for half in range(2):
                    home_copy(d, a, kv, half).start()

    def own_copy(a, kv, half, device):
        return remote(
            own_out.at[a, kv, half], home_in.at[y, 2, a, kv], sem_os.at[a, kv, half], sem_hr.at[y, 2, a, kv], device
        )

    def own_send(a):
        for kv in range(2):
            for half in range(2):
                own_out[a, kv, half] = dkv[a, z, kv, half * FEAT : (half + 1) * FEAT].astype(BF16)

            @pl.when(first_half)
            def _():
                own_copy(a, kv, yo, (b, 2 * z + yo)).start()

            @pl.when(later_half)
            def _():
                for half in range(2):
                    own_copy(a, kv, half, (prv, 2 * z + half)).start()

    def dq_send(a):
        return remote(dq_out.at[a], dq_in.at[a], sem_dqs.at[a], sem_dqr.at[a], partner)

    def dq_cols(who, a):
        return dq_hbm.at[:, span((2 * who + a) * 1024, 1024)]

    def dq_away(a):
        for h in range(8):
            dq_out[a, h] = (dq_t[a, yo, :, h * FEAT : (h + 1) * FEAT].T * SCALE).astype(BF16)
        dq_send(a).start()

    def dq_keep(a):
        for h in range(8):
            dq_stage[0, a, :, h * FEAT : (h + 1) * FEAT] = dq_t[a, y, :, h * FEAT : (h + 1) * FEAT].T * SCALE
        pltpu.make_async_copy(dq_stage.at[0, a], dq_cols(y, a), sem_out.at[0, a]).start()

    def dq_back(a):
        dq_send(a).wait_recv()
        for h in range(8):
            dq_stage[1, a, :, h * FEAT : (h + 1) * FEAT] = dq_in[a, h].astype(F32)
        pltpu.make_async_copy(dq_stage.at[1, a], dq_cols(yo, a), sem_out.at[1, a]).start()

    def partner_rows(a):
        for g in range(4 * a, 4 * a + 4):
            _, quad, t, (_, dst) = q_part(g)
            place = dst.at[a, yo, pl.ds(4 * quad, 4)]
            pltpu.make_async_copy(place, place, sem_qr.at[a, t, quad]).wait()

    def landed(pair, part, a, kv):
        place = home_in.at[pair, part, a, kv]
        pltpu.make_async_copy(place, place, sem_hr.at[pair, part, a, kv]).wait()
        return home_in[pair, part, a, kv].astype(F32)

    def finish(a):
        for kv, (ref, factor) in ((1, (dv_hbm, 1.0)), (0, (dk_hbm, SCALE))):
            for who, pair in enumerate((y, yo)):
                total = landed(pair, 0, a, kv) + landed(pair, 1, a, kv)
                mine = first_half if who == 0 else False

                @pl.when(mine)
                def _():
                    fin[who, a, kv] = (total + dkv[a, z, kv, span(y * FEAT, FEAT)]) * factor

                @pl.when(jnp.logical_not(mine))
                def _():
                    fin[who, a, kv] = (total + landed(pair, 2, a, kv)) * factor

                pltpu.make_async_copy(
                    fin.at[who, a, kv], ref.at[:, span((2 * pair + a) * FEAT, FEAT)], sem_fin.at[who, a, kv]
                ).start()

    before_unit = {
        0: lambda: (gather_on(0), gather_on(1), gather_on(2)),
        1: lambda: (gather_on(3), q_next(0)),
        2: lambda: (gather_on(4), q_next(1), gather_on(5), gather_on(6)),
        3: lambda: (gather_on(7), q_next(2)),
        4: lambda: (gather_on(8), q_next(3), st_send.wait_recv(), partner_rows(0)),
        5: lambda: gather_on(9),
        6: lambda: (gather_on(10), q_next(4)),
        7: lambda: gather_on(11),
        8: lambda: (q_next(5), gather_on(12), gather_on(13), gather_on(14)),
        10: lambda: gather_on(15),
        11: lambda: partner_rows(1),
    }
    after_unit = {
        7: lambda: reduce_step(1, 0, 0),
        9: lambda: (reduce_step(0, 0, 0), dq_away(0), own_send(0)),
        10: lambda: (reduce_step(1, 0, 1), dq_keep(0), dq_keep(1)),
        11: lambda: (reduce_step(1, 1, 0), reduce_step(0, 0, 1), own_send(1)),
        12: lambda: (reduce_step(0, 1, 0), reduce_step(1, 0, 2)),
        13: lambda: (reduce_step(1, 1, 1), reduce_step(0, 0, 2)),
        14: lambda: (reduce_step(0, 1, 1), dq_away(1), reduce_step(1, 1, 2), reduce_step(0, 0, 3)),
    }

    def unit_step(n, carry):
        for at, action in before_unit.items():
            pl.when(n == at)(lambda action=action: (action(), None)[1])
        chunks = tuple(
            (pick(n, [u[c][0] for u in UNITS]), (z + 8 + pick(n, [u[c][1] for u in UNITS])) % 8)
            for c in range(2)
        )
        away = pick(n, [int(u[2]) for u in UNITS])
        src = jnp.where(away == 1, yo, y)
        masked = jnp.where(jnp.logical_and(chunks[1][1] == z, first_half), 1 + src, 0)
        pair_unit(src, chunks, (None, masked))
        for at, action in after_unit.items():
            pl.when(n == at)(lambda action=action: (action(), None)[1])
        return carry

    lax.fori_loop(0, len(UNITS), unit_step, 0)

    reduce_step(0, 1, 2)
    reduce_step(1, 1, 3)
    dq_back(0)
    finish(0)
    dq_back(1)
    finish(1)

    q_sent(6)
    q_sent(7)
    for a in range(2):
        for kv in range(2):
            place = kv_s.at[a, 0, 0, kv]
            pltpu.make_async_copy(place, place, sem_as.at[0, a, kv]).wait()

            @pl.when(first_half)
            def _():
                own_copy(a, kv, yo, partner).wait_send()

            @pl.when(later_half)
            def _():
                pltpu.make_async_copy(place, place, sem_as.at[1, a, kv]).wait()
                for half in range(2):
                    own_copy(a, kv, half, partner).wait_send()

            for who in range(2):
                pltpu.make_async_copy(fin.at[who, a, kv], fin.at[who, a, kv], sem_fin.at[who, a, kv]).wait()
        for d in range(2):
            steps = 4 if d == a else 3
            for half in range(2):
                for s in range(steps):
                    gather_copy(d, a, s, half).wait_send()
                for kv in range(2):
                    home_copy(d, a, kv, half).wait_send()
            for kv in range(2):
                for s in range(steps - 1):
                    reduce_copy(d, a, s, kv).wait_send()
        dq_send(a).wait_send()
        for who, device in enumerate((y, yo)):
            pltpu.make_async_copy(dq_stage.at[who, a], dq_cols(device, a), sem_out.at[who, a]).wait()
    st_send.wait_send()


def settle(*refs):
    sources, results, held, sems = refs[0:3], refs[3:6], refs[6:9], refs[9]
    loads, stores = [], []
    for src, mid, dst, parts in zip(sources, held, results, (8, 2, 2)):
        rows = src.shape[0] // parts
        for i in range(parts):
            at = pl.ds(i * rows, rows)
            n = len(loads)
            loads.append(pltpu.make_async_copy(src.at[at], mid.at[at], sems.at[0, n]))
            stores.append(pltpu.make_async_copy(mid.at[at], dst.at[at], sems.at[1, n]))
    for load in loads:
        load.start()
    for load, store in zip(loads, stores):
        load.wait()
        store.start()
    for store in stores:
        store.wait()


def core(queries, key_matrix, value_matrix, saved_output, output_gradient, saved_logsumexp, block_order):
    dma = pltpu.SemaphoreType.DMA
    vmem = pltpu.VMEM
    hbm = pl.BlockSpec(memory_space=pltpu.HBM)
    shapes = [
        jax.ShapeDtypeStruct(array.shape, F32) for array in (queries, key_matrix, value_matrix)
    ]
    gradients = pl.pallas_call(
        kernel,
        out_shape=shapes,
        in_specs=[hbm] * 7,
        out_specs=[hbm] * 3,
        scratch_shapes=[
            pltpu.SMEM((32,), jnp.int32),
            vmem((2, 2, 8, 128, 128), BF16),
            vmem((2, 2, 8, 128, 128), BF16),
            vmem((2, 8, 2, 2, 128, 128), BF16),
            vmem((128, 4096), BF16),
            vmem((128, 4096), BF16),
            vmem((32, 128), F32),
            vmem((2, 32, 128), F32),
            vmem((2, 2, 16, 128), F32),
            vmem((3, 256, 256), F32),
            vmem((2, 256, 1024), BF16),
            vmem((2, 256, 1024), BF16),
            vmem((2, 2, 128, 1024), F32),
            vmem((2, 8, 2, 256, 128), F32),
            vmem((2, 2, 3, 2, 2, 128, 128), BF16),
            vmem((2, 2, 4, 2, 2, 128, 128), BF16),
            vmem((2, 2, 2, 128, 128), BF16),
            vmem((2, 3, 2, 2, 128, 128), BF16),
            vmem((2, 2, 2, 128, 128), F32),
            vmem((2, 8, 128, 128), BF16),
            vmem((2, 8, 128, 128), BF16),
            vmem((2, 2, 128, 1024), F32),
            dma((4,)),
            dma((2, 2)),
            dma((2, 2, 2)),
            dma((2, 2, 2)),
            dma((2,)),
            dma((2, 2, 2)),
            dma((2, 2, 2)),
            dma((2, 2, 4, 2)),
            dma((2, 2, 4, 2)),
            dma((2, 2, 3, 2)),
            dma((2, 2, 3, 2)),
            dma((2, 3, 2, 2)),
            dma((2, 2, 2, 2)),
            dma((2, 2, 2)),
            dma((2, 2, 2)),
            dma((2,)),
            dma((2,)),
            dma((2, 2)),
        ],
        compiler_params=pltpu.CompilerParams(
            collective_id=0, has_side_effects=True, vmem_limit_bytes=62 << 20
        ),
        name="attention_backward",
    )(
        block_order, queries, key_matrix, value_matrix, saved_output, output_gradient, saved_logsumexp.T
    )
    return pl.pallas_call(
        settle,
        out_shape=shapes,
        in_specs=[hbm] * 3,
        out_specs=[hbm] * 3,
        scratch_shapes=[vmem(shape.shape, F32) for shape in shapes] + [dma((2, 12))],
        compiler_params=pltpu.CompilerParams(vmem_limit_bytes=62 << 20),
        name="settle",
    )(*gradients)


def solution(mesh):
    rows = P(("blk", "head"), None)
    return jax.shard_map(
        core,
        mesh=mesh,
        in_specs=(rows,) * 6 + (P(),),
        out_specs=(rows,) * 3,
        check_vma=False,
    )
```
